128 devices in a mesh: group: 4 (over y), member: 32 (over x, z, core).
Axes of the slice: x: 4, y: 4, z: 4, core: 2. Of those that a mesh axis runs over, the one named last changes fastest.
Arguments:
- values: bfloat16 [4096, 16, 128, 128], P(('group', 'member')), may hold values from -6 to 6
- block_ids: int32 [4096, 16], P(('group', 'member')), may hold values from 0 to 4095, as said below
- target: float32 [4096, 128], P(('group', 'member')), may hold values from -6 to 6
- table: bfloat16 [4096, 128, 256], P(('group', 'member')), may hold values from -0.03125 to 0.03125
- linear: bfloat16 [4096, 128], P(('group', 'member')), may hold values from -0.125 to 0.125
- block_class: int32 [4096], P(('group', 'member')), may hold values from 0 to 256, as said below
Outputs:
- emb_grad: float32 [4096, 128, 256], P(('group', 'member'))
- lin_grad: float32 [4096, 128], P(('group', 'member'))
- residual: float32 [4096, 128], P(('group', 'member'))
The draws below stay inside these ranges and needn't reach their ends.
Inputs may be any that keep to these rules, and one draw needn't show every extreme that they name: `block_ids`: each tile's 16 blocks have 16 different owners, the owner of block b being b // 32; all blocks of one owner named in the tiles of one device are the same block. `block_class`: each value is 0, 64 or 256.
All inputs are finite; a program needn't handle non-finite values.
Results may differ from the reference program's by a relative error of at most 0.0043.
Values may be sent and summed in bfloat16 or wider, within the bound.
No kernel may reach another device: no remote copies, remote signals or barrier semaphores. Data moves between devices by JAX's collectives and lax.ppermute only.
A program may use at most 192 MiB of HBM per device.

```python
import jax
import jax.numpy as jnp
from jax import lax

EMB = 256
BROWS = 128
TSAMP = 128
K = 16
TILES_DEV = 32
BLK_DEV = 32
TILES = 4096
BLOCKS = 4096
N_GROUP = 4
N_MEMBER = 32


def draw_block_ids(key, part):
    key = jax.random.fold_in(key, 11)
    peers = N_GROUP * N_MEMBER
    key_pop, key_loc, key_score = jax.random.split(key, 3)
    popular = jax.random.randint(key_pop, (peers,), 1, 9)
    found_position = jax.random.randint(key_loc, (peers, peers), 0, BLK_DEV)
    found_position = found_position.at[0, peers - 1].set(BLK_DEV - 1)
    found_position = found_position.at[0, 0].set(0)
    ranking_scores = jax.random.randint(key_score, (TILES, peers), 0, 65536) * popular[None, :]
    ranking_scores = ranking_scores * peers + jnp.arange(peers, dtype=jnp.int32)[None, :]
    leading_tile = jnp.arange(TILES, dtype=jnp.int32) % TILES_DEV == 0
    owner_ids = jnp.arange(peers, dtype=jnp.int32)
    mandatory_pick = (owner_ids == 0) | (owner_ids == peers - 1)
    extra_boost = jnp.where(leading_tile[:, None] & mandatory_pick[None, :], 2 ** 27, 0)
    ranking_scores = (ranking_scores + extra_boost).astype(jnp.int32)
    _, owners = lax.top_k(ranking_scores, K)
    device_of = jnp.arange(TILES, dtype=jnp.int32) // TILES_DEV
    local_index = found_position[device_of[:, None], owners]
    return (owners * BLK_DEV + local_index).astype(jnp.int32)


def draw_block_class(key, part):
    key = jax.random.fold_in(key, 23)
    picks = jax.random.randint(key, (BLOCKS,), 0, 4)
    classes = jnp.where(picks == 0, 0, jnp.where(picks == 3, 256, 64))
    classes = classes.at[0].set(0).at[BLOCKS - 1].set(256)
    return classes.astype(jnp.int32)


def block_scale(key, shape, pieces, low, top_value):
    def one(dim, parts):
        heights = jax.random.uniform(jax.random.fold_in(jax.random.fold_in(key, 6), dim), (parts,), jnp.float32, low / len(pieces), top_value / len(pieces))
        return jnp.repeat(jnp.exp(heights), shape[dim] // parts).reshape((-1,) + (1,) * (len(shape) - dim - 1))

    level = one(*pieces[0])
    for cut in pieces[1:]:
        level = level * one(*cut)
    return level


def scatter_about(own_key, extent, width, most, shards=(), kind=jnp.bfloat16):
    array = jax.random.normal(own_key, extent, jnp.float32) * width
    if len(shards) > 0:
        array = block_scale(own_key, extent, shards, -0.22, 0.18) * array
    return jnp.clip(array, min=-most, max=most).astype(kind)


def setup_inputs(seed: int = 0) -> dict:
    key_list = jax.random.split(jax.random.key(seed), 7)
    return {
        "values": scatter_about(key_list[0], (TILES, K, TSAMP, BROWS), 1.0, 6.0, ((0, 128),)),
        "block_ids": draw_block_ids(jax.random.fold_in(key_list[6], 71), 0),
        "target": scatter_about(key_list[2], (TILES, TSAMP), 1.0, 6.0, ((0, 128),), jnp.float32),
        "table": scatter_about(key_list[3], (BLOCKS, BROWS, EMB), (K * BROWS * 16) ** -0.5, 0.03125, ((0, 128),)),
        "linear": scatter_about(key_list[4], (BLOCKS, BROWS), (K * BROWS) ** -0.5, 0.125, ((0, 128),)),
        "block_class": draw_block_class(jax.random.fold_in(key_list[6], 71), 0),
    }


def reference(values, block_ids, target, table, linear, block_class):
    col_mask = jnp.arange(EMB)[None, :] < block_class[:, None]
    factors = jnp.where(col_mask[:, None, :], table, jnp.zeros_like(table))
    gscale = (TSAMP * TILES_DEV * K / BLK_DEV) ** -0.5

    def one_tile(carry, inputs):
        acc_emb, acc_lin = carry
        tile_vals, tile_ids, tile_target = inputs
        picked = factors[tile_ids].astype(jnp.float32)
        picked_lin = linear[tile_ids].astype(jnp.float32)
        vals_f = tile_vals.astype(jnp.float32)
        sq_vals = (vals_f * vals_f).astype(jnp.bfloat16).astype(jnp.float32)
        sq_fac = (picked * picked).astype(jnp.bfloat16).astype(jnp.float32)
        sums = jnp.einsum('ksf,kfd->sd', vals_f, picked)
        squares = jnp.einsum('ksf,kfd->sd', sq_vals, sq_fac)
        lin_part = jnp.einsum('ksf,kf->s', vals_f, picked_lin)
        resid = lin_part + 0.5 * jnp.sum(sums * sums - squares, axis=1) - tile_target
        scaled = resid * gscale
        scaled_b = scaled.astype(jnp.bfloat16).astype(jnp.float32)
        weighted = (scaled[:, None] * sums).astype(jnp.bfloat16).astype(jnp.float32)
        term = jnp.einsum('ksf,sd->kfd', vals_f, weighted)
        term = term - jnp.einsum('ksf,s->kf', sq_vals, scaled_b)[:, :, None] * picked
        lin_term = jnp.einsum('ksf,s->kf', vals_f, scaled_b)
        acc_emb = acc_emb.at[tile_ids].add(term)
        acc_lin = acc_lin.at[tile_ids].add(lin_term)
        return (acc_emb, acc_lin), resid

    start = (jnp.zeros((BLOCKS, BROWS, EMB), jnp.float32), jnp.zeros((BLOCKS, BROWS), jnp.float32))
    (acc_emb, acc_lin), residual = lax.scan(one_tile, start, (values, block_ids.astype(jnp.int32), target))
    emb_grad = acc_emb * col_mask[:, None, :].astype(jnp.float32)
    return emb_grad, acc_lin, residual
```

```python
import jax
import jax.numpy as jnp
from jax import lax
from jax.experimental import pallas as pl
from jax.experimental.pallas import tpu as pltpu
from jax.sharding import PartitionSpec as P

AXES = ("group", "member")
EXTRA = 16
NT = (((1,), (1,)), ((), ()))
NN = (((1,), (0,)), ((), ()))
F32 = jnp.float32
BF16 = jnp.bfloat16


def swap(x):
    return lax.all_to_all(x, AXES, split_axis=0, concat_axis=0, tiled=True)


def prepare_body(cls_ref, table_ref, lin_ref, out_ref):
    step = pl.program_id(0)
    per = table_ref.shape[0]
    brows, cols = table_ref.shape[1:]
    for i in range(per):
        width = cls_ref[step * per + i]
        row = lax.broadcasted_iota(jnp.int32, (cols, brows), 0)
        vt = jnp.where(row < width, table_ref[i].astype(F32).T, 0.0)
        sq = (vt * vt).astype(BF16).astype(F32)
        total = jnp.sum(sq, axis=0, keepdims=True)
        hi = total.astype(BF16).astype(F32)
        mid = (total - hi).astype(BF16).astype(F32)
        low = total - hi - mid
        at = lax.broadcasted_iota(jnp.int32, (EXTRA, brows), 0)
        extra = jnp.where(at == 0, lin_ref[i].astype(F32), 0.0)
        extra = jnp.where(at == 1, hi, extra)
        extra = jnp.where(at == 2, mid, extra)
        extra = jnp.where(at == 3, low, extra)
        out_ref[i, :cols] = vt.astype(BF16)
        out_ref[i, cols:] = extra.astype(BF16)


def prepare(table, linear, block_class):
    blocks, brows, cols = table.shape
    per = 8
    return pl.pallas_call(
        prepare_body,
        grid=(blocks // per,),
        in_specs=[
            pl.BlockSpec(memory_space=pltpu.SMEM),
            pl.BlockSpec((per, brows, cols), lambda i: (i, 0, 0)),
            pl.BlockSpec((per, 1, brows), lambda i: (i, 0, 0)),
        ],
        out_specs=pl.BlockSpec((per, cols + EXTRA, brows), lambda i: (i, 0, 0)),
        out_shape=jax.ShapeDtypeStruct((blocks, cols + EXTRA, brows), BF16),
        cost_estimate=pl.CostEstimate(flops=1 << 24, bytes_accessed=1 << 22, transcendentals=0),
        name="prepare",
    )(block_class, table, linear.reshape(blocks, 1, brows))


def pick_body(idx_ref, rows_ref, out_ref, sem):
    peers = out_ref.shape[0]

    @pl.loop(0, peers)
    def _(p):
        pltpu.make_async_copy(rows_ref.at[idx_ref[p]], out_ref.at[p], sem).start()

    pltpu.make_async_copy(out_ref, out_ref, sem).wait()


def pick(idx, rows):
    peers = idx.shape[0]
    return pl.pallas_call(
        pick_body,
        in_specs=[
            pl.BlockSpec(memory_space=pltpu.SMEM),
            pl.BlockSpec(memory_space=pltpu.VMEM),
        ],
        out_specs=pl.BlockSpec(memory_space=pl.ANY),
        out_shape=jax.ShapeDtypeStruct((peers, *rows.shape[1:]), rows.dtype),
        scratch_shapes=[pltpu.SemaphoreType.DMA],
        name="pick",
    )(idx, rows)


def tiles_body(gscale, own_ref, x_ref, pulled_ref, target_ref, out_ref, resid_ref, acc_ref):
    t = pl.program_id(0)
    steps = pl.num_programs(0)
    per_tile, tsamp, brows = x_ref.shape[1:]
    peers, rows, _ = pulled_ref.shape
    cols = rows - EXTRA

    @pl.when(t == 0)
    def _():
        @pl.loop(0, peers)
        def _(o):
            acc_ref[o] = jnp.zeros((rows, brows), F32)

    sums = jnp.zeros((rows, tsamp), F32)
    squares = jnp.zeros((EXTRA, tsamp), F32)
    for k in range(0, per_tile, 2):
        a, b = own_ref[t, k], own_ref[t, k + 1]
        x = jnp.concatenate([x_ref[0, k], x_ref[0, k + 1]], axis=1)
        v = jnp.concatenate([pulled_ref[a], pulled_ref[b]], axis=1)
        sums = sums + lax.dot_general(v, x, NT, preferred_element_type=F32)
        squares = squares + lax.dot_general(v[cols:], x * x, NT, preferred_element_type=F32)
    main = sums[:cols]
    square = squares[1:2] + squares[2:3] + squares[3:4]
    inter = jnp.sum(main * main, axis=0, keepdims=True)
    resid = sums[cols : cols + 1] + 0.5 * (inter - square) - target_ref[pl.ds(t, 1), :]
    resid_ref[pl.ds(t, 1), :] = resid
    scaled = resid * gscale
    weighted = (main * scaled).astype(BF16)
    at = lax.broadcasted_iota(jnp.int32, (EXTRA, tsamp), 0)
    lin_lhs = jnp.where(at == 0, scaled, 0.0).astype(BF16)
    sq_lhs = jnp.where(at == 1, scaled, 0.0).astype(BF16)
    for k in range(0, per_tile, 2):
        a, b = own_ref[t, k], own_ref[t, k + 1]
        x = jnp.concatenate([x_ref[0, k], x_ref[0, k + 1]], axis=1)
        term = lax.dot_general(weighted, x, NN, preferred_element_type=F32)
        rest = lax.dot_general(lin_lhs, x, NN, preferred_element_type=F32)
        rest = rest + lax.dot_general(sq_lhs, x * x, NN, preferred_element_type=F32)
        for o, part in ((a, slice(0, brows)), (b, slice(brows, 2 * brows))):
            acc_ref[o, :cols] += term[:, part]
            acc_ref[o, cols:] += rest[:, part]

    @pl.when(t == steps - 1)
    def _():
        @pl.loop(0, peers)
        def _(o):
            out_ref[o, :cols] = acc_ref[o, :cols].astype(BF16)
            extra = acc_ref[o, cols:]
            hi = extra.astype(BF16).astype(F32)
            out_ref[o, cols:] = (hi + pltpu.roll(extra - hi, 2, 0)).astype(BF16)


def tiles(owners, values, pulled, target, gscale):
    n_tiles, per_tile, tsamp, brows = values.shape
    peers, rows, _ = pulled.shape
    return pl.pallas_call(
        lambda *refs: tiles_body(gscale, *refs),
        grid=(n_tiles,),
        in_specs=[
            pl.BlockSpec(memory_space=pltpu.SMEM),
            pl.BlockSpec((1, per_tile, tsamp, brows), lambda t: (t, 0, 0, 0)),
            pl.BlockSpec(memory_space=pltpu.VMEM),
            pl.BlockSpec(memory_space=pltpu.VMEM),
        ],
        out_specs=[
            pl.BlockSpec(memory_space=pltpu.VMEM),
            pl.BlockSpec(memory_space=pltpu.VMEM),
        ],
        out_shape=[
            jax.ShapeDtypeStruct((peers, rows, brows), BF16),
            jax.ShapeDtypeStruct((n_tiles, tsamp), F32),
        ],
        scratch_shapes=[pltpu.VMEM((peers, rows, brows), F32)],
        compiler_params=pltpu.CompilerParams(vmem_limit_bytes=60 << 20),
        name="tiles",
    )(owners, values, pulled, target)


def reduce_body(idx_ref, cls_ref, recv_ref, rows_ref, emb_ref, lin_ref, acc_ref):
    step = pl.program_id(0)
    per = recv_ref.shape[0]
    blocks, rows, brows = acc_ref.shape
    cols = rows - EXTRA

    @pl.when(step == 0)
    def _():
        @pl.loop(0, blocks)
        def _(j):
            acc_ref[j] = jnp.zeros((rows, brows), F32)

    for i in range(per):
        j = idx_ref[step * per + i]
        acc_ref[j] += recv_ref[i].astype(F32)

    @pl.when(step == pl.num_programs(0) - 1)
    def _():
        @pl.loop(0, blocks)
        def _(j):
            extra = acc_ref[j, cols:]
            lin_ref[pl.ds(j, 1), :] = extra[0:1] + extra[2:3]
            decay = extra[1:2] + extra[3:4]
            grad = acc_ref[j, :cols] - decay * rows_ref[j, :cols].astype(F32)
            row = lax.broadcasted_iota(jnp.int32, (cols, brows), 0)
            emb_ref[j] = jnp.where(row < cls_ref[j], grad, 0.0).T


def reduce_grads(idx, block_class, recv, rows_t):
    peers, rows, brows = recv.shape
    blocks = block_class.shape[0]
    cols = rows - EXTRA
    per = 16
    return pl.pallas_call(
        reduce_body,
        grid=(peers // per,),
        in_specs=[
            pl.BlockSpec(memory_space=pltpu.SMEM),
            pl.BlockSpec(memory_space=pltpu.SMEM),
            pl.BlockSpec((per, rows, brows), lambda i: (i, 0, 0)),
            pl.BlockSpec(memory_space=pltpu.VMEM),
        ],
        out_specs=[
            pl.BlockSpec(memory_space=pltpu.VMEM),
            pl.BlockSpec(memory_space=pltpu.VMEM),
        ],
        out_shape=[
            jax.ShapeDtypeStruct((blocks, brows, cols), F32),
            jax.ShapeDtypeStruct((blocks, brows), F32),
        ],
        scratch_shapes=[pltpu.VMEM((blocks, rows, brows), F32)],
        compiler_params=pltpu.CompilerParams(vmem_limit_bytes=40 << 20),
        name="reduce_grads",
    )(idx, block_class, recv, rows_t)


def on_device(values, block_ids, target, table, linear, block_class):
    peers = lax.axis_size("group") * lax.axis_size("member")
    blk_dev = table.shape[0]
    n_tiles, per_tile, tsamp, _ = values.shape
    gscale = (tsamp * n_tiles * per_tile / blk_dev) ** (-0.5)
    owners = block_ids // blk_dev
    local_index = block_ids % blk_dev
    matches = owners.reshape(-1)[:, None] == jnp.arange(peers, dtype=jnp.int32)[None, :]
    wanted = jnp.max(jnp.where(matches, local_index.reshape(-1)[:, None], 0), axis=0)
    idx = swap(wanted.reshape(peers, 1)).reshape(peers)
    rows_t = prepare(table, linear, block_class)
    pulled = swap(pick(idx, rows_t))
    acc, residual = tiles(owners, values, pulled, target, gscale)
    recv = swap(acc)
    emb_grad, lin_grad = reduce_grads(idx, block_class, recv, rows_t)
    return emb_grad, lin_grad, residual


def solution(mesh):
    return jax.shard_map(
        on_device,
        mesh=mesh,
        in_specs=(
            P(AXES, None, None, None),
            P(AXES, None),
            P(AXES, None),
            P(AXES, None, None),
            P(AXES, None),
            P(AXES),
        ),
        out_specs=(P(AXES, None, None), P(AXES, None), P(AXES, None)),
        check_vma=False,
    )
```

```python
import jax
import jax.numpy as jnp
from jax import lax
from jax.experimental import pallas as pl
from jax.experimental.pallas import tpu as pltpu
from jax.sharding import PartitionSpec as P

AXES = ("group", "member")
EXTRA = 8
NT = (((1,), (1,)), ((), ()))
NN = (((1,), (0,)), ((), ()))
F32 = jnp.float32
BF16 = jnp.bfloat16


def swap(x):
    return lax.all_to_all(x, AXES, split_axis=0, concat_axis=0, tiled=True)


def prepare_body(cls_ref, table_ref, lin_ref, out_ref, lin32_ref):
    blocks, brows, cols = table_ref.shape
    lin32_ref[...] = lin_ref[...].astype(F32)
    one = lax.broadcasted_iota(jnp.int32, (cols, cols), 0)
    one = jnp.where(one == lax.broadcasted_iota(jnp.int32, (cols, cols), 1), 1.0, 0.0).astype(BF16)
    row = lax.broadcasted_iota(jnp.int32, (cols, brows), 0)
    at = lax.broadcasted_iota(jnp.int32, (EXTRA, brows), 0)

    @pl.loop(0, blocks, unroll=4)
    def _(j):
        vt = lax.dot_general(one, table_ref[j], NT, preferred_element_type=F32)
        vt = jnp.where(row < cls_ref[j], vt, 0.0)
        total = jnp.sum((vt * vt).astype(BF16).astype(F32), axis=0, keepdims=True)
        hi = total.astype(BF16).astype(F32)
        mid = (total - hi).astype(BF16).astype(F32)
        low = total - hi - mid
        extra = jnp.where(at == 0, lin32_ref[pl.ds(j, 1), :], 0.0)
        extra = jnp.where(at == 1, hi, extra)
        extra = jnp.where(at == 2, mid, extra)
        extra = jnp.where(at == 3, low, extra)
        out_ref[j] = jnp.concatenate([vt, extra], axis=0).astype(BF16)


def prepare(table, linear, block_class):
    blocks, brows, cols = table.shape
    whole = pl.BlockSpec(memory_space=pltpu.VMEM)
    return pl.pallas_call(
        prepare_body,
        in_specs=[pl.BlockSpec(memory_space=pltpu.SMEM), whole, whole],
        out_specs=whole,
        out_shape=jax.ShapeDtypeStruct((blocks, cols + EXTRA, brows), BF16),
        scratch_shapes=[pltpu.VMEM(linear.shape, F32)],
        compiler_params=pltpu.CompilerParams(vmem_limit_bytes=16 << 20),
        cost_estimate=pl.CostEstimate(flops=1 << 24, bytes_accessed=1 << 22, transcendentals=0),
        name="prepare",
    )(block_class, table, linear)


def pick_body(idx_ref, rows_ref, out_ref):
    @pl.loop(0, out_ref.shape[0], unroll=2)
    def _(p):
        out_ref[p] = rows_ref[idx_ref[p, 0, 0]]


def pick(idx, rows):
    peers = idx.shape[0]
    whole = pl.BlockSpec(memory_space=pltpu.VMEM)
    return pl.pallas_call(
        pick_body,
        in_specs=[pl.BlockSpec(memory_space=pltpu.SMEM), whole],
        out_specs=whole,
        out_shape=jax.ShapeDtypeStruct((peers, *rows.shape[1:]), rows.dtype),
        compiler_params=pltpu.CompilerParams(vmem_limit_bytes=24 << 20),
        name="pick",
    )(idx, rows)


def tiles_body(gscale, own_ref, x_ref, pulled_ref, target_ref, out_ref, resid_ref, acc_ref):
    step = pl.program_id(0)
    per, per_tile, tsamp, brows = x_ref.shape
    peers, rows, _ = pulled_ref.shape
    cols = rows - EXTRA

    @pl.when(step == 0)
    def _():
        @pl.loop(0, peers)
        def _(o):
            acc_ref[o] = jnp.zeros((rows, brows), F32)

    def square(x):
        return (x * x).astype(F32)

    at = lax.broadcasted_iota(jnp.int32, (EXTRA, tsamp), 0)
    left = []
    for i in range(per):
        t = step * per + i
        sums = [jnp.zeros((rows, tsamp), F32)] * 2
        squares = jnp.zeros((tsamp, brows), F32)
        for k in range(0, per_tile, 2):
            n = (k // 2) % 2
            va, vb = pulled_ref[own_ref[t, k]], pulled_ref[own_ref[t, k + 1]]
            xa, xb = x_ref[i, k], x_ref[i, k + 1]
            v = jnp.concatenate([va, vb], axis=1)
            x = jnp.concatenate([xa, xb], axis=1)
            sums[n] += lax.dot_general(v, x, NT, preferred_element_type=F32)
            for vk, xk in ((va, xa), (vb, xb)):
                rest = vk[cols:].astype(F32)
                squares += square(xk) * (rest[1:2] + rest[2:3] + rest[3:4])
        total = sums[0] + sums[1]
        main = total[:cols]
        sub = jnp.sum(squares.T, axis=0, keepdims=True)
        inter = jnp.sum(main * main, axis=0, keepdims=True)
        resid = total[cols : cols + 1] + 0.5 * (inter - sub) - target_ref[pl.ds(t, 1), :]
        resid_ref[pl.ds(t, 1), :] = resid
        scaled = resid * gscale
        lin = jnp.where(at == 0, scaled, 0.0)
        decay = jnp.where(at == 1, scaled, 0.0)
        of_x = jnp.concatenate([main * scaled, lin], axis=0).astype(BF16)
        of_sq = jnp.concatenate([jnp.zeros((cols, tsamp), F32), decay], axis=0).astype(BF16)
        left.append(jnp.concatenate([of_x, of_sq], axis=1))
    for i in range(per):
        t = step * per + i
        for k in range(0, per_tile, 2):
            x = jnp.concatenate([x_ref[i, k], x_ref[i, k + 1]], axis=1)
            both = jnp.concatenate([x, x * x], axis=0)
            term = lax.dot_general(left[i], both, NN, preferred_element_type=F32)
            acc_ref[own_ref[t, k]] += term[:, :brows]
            acc_ref[own_ref[t, k + 1]] += term[:, brows:]

    @pl.when(step == pl.num_programs(0) - 1)
    def _():
        @pl.loop(0, peers)
        def _(o):
            extra = acc_ref[o, cols:]
            hi = extra.astype(BF16).astype(F32)
            extra = hi + pltpu.roll(extra - hi, 2, 0)
            out_ref[o] = jnp.concatenate([acc_ref[o, :cols], extra], axis=0).astype(BF16)


def tiles(owners, values, pulled, target, gscale):
    n_tiles, per_tile, tsamp, brows = values.shape
    peers, rows, _ = pulled.shape
    per = 4
    return pl.pallas_call(
        lambda *refs: tiles_body(gscale, *refs),
        grid=(n_tiles // per,),
        in_specs=[
            pl.BlockSpec(memory_space=pltpu.SMEM),
            pl.BlockSpec((per, per_tile, tsamp, brows), lambda t: (t, 0, 0, 0)),
            pl.BlockSpec(memory_space=pltpu.VMEM),
            pl.BlockSpec(memory_space=pltpu.VMEM),
        ],
        out_specs=[
            pl.BlockSpec(memory_space=pltpu.VMEM),
            pl.BlockSpec(memory_space=pltpu.VMEM),
        ],
        out_shape=[
            jax.ShapeDtypeStruct((peers, rows, brows), BF16),
            jax.ShapeDtypeStruct((n_tiles, tsamp), F32),
        ],
        scratch_shapes=[pltpu.VMEM((peers, rows, brows), F32)],
        compiler_params=pltpu.CompilerParams(vmem_limit_bytes=28 << 20),
        name="tiles",
    )(owners, values, pulled, target)


def reduce_body(idx_ref, cls_ref, recv_ref, rows_ref, emb_ref, lin_ref, acc_ref, done_ref, sem):
    peers = recv_ref.shape[0]
    blocks, rows, brows = acc_ref.shape
    cols = rows - EXTRA

    @pl.loop(0, blocks)
    def _(j):
        acc_ref[j] = jnp.zeros((rows, brows), F32)

    @pl.loop(0, peers, unroll=2)
    def _(p):
        j = idx_ref[p, 0, 0]
        acc_ref[j] += recv_ref[p].astype(F32)

    row = lax.broadcasted_iota(jnp.int32, (cols, brows), 0)

    @pl.loop(0, blocks, unroll=2)
    def _(j):
        extra = acc_ref[j, cols:]
        lin_ref[pl.ds(j, 1), :] = extra[0:1] + extra[2:3]
        decay = extra[1:2] + extra[3:4]
        grad = acc_ref[j, :cols] - decay * rows_ref[j].astype(F32)[:cols]
        done_ref[j] = jnp.where(row < cls_ref[j], grad, 0.0).T
        pltpu.make_async_copy(done_ref.at[j], emb_ref.at[j], sem).start()

    pltpu.make_async_copy(done_ref, emb_ref, sem).wait()


def reduce_grads(idx, block_class, recv, rows_t):
    peers, rows, brows = recv.shape
    blocks = block_class.shape[0]
    cols = rows - EXTRA
    scalars = pl.BlockSpec(memory_space=pltpu.SMEM)
    whole = pl.BlockSpec(memory_space=pltpu.VMEM)
    return pl.pallas_call(
        reduce_body,
        in_specs=[scalars, scalars, whole, whole],
        out_specs=[pl.BlockSpec(memory_space=pl.ANY), whole],
        out_shape=[
            jax.ShapeDtypeStruct((blocks, brows, cols), F32),
            jax.ShapeDtypeStruct((blocks, brows), F32),
        ],
        scratch_shapes=[
            pltpu.VMEM((blocks, rows, brows), F32),
            pltpu.VMEM((blocks, brows, cols), F32),
            pltpu.SemaphoreType.DMA,
        ],
        compiler_params=pltpu.CompilerParams(vmem_limit_bytes=24 << 20),
        name="reduce_grads",
    )(idx, block_class, recv, rows_t)


def on_device(values, block_ids, target, table, linear, block_class):
    peers = lax.axis_size("group") * lax.axis_size("member")
    blk_dev = table.shape[0]
    n_tiles, per_tile, tsamp, _ = values.shape
    gscale = (tsamp * n_tiles * per_tile / blk_dev) ** (-0.5)
    owners = block_ids // blk_dev
    local_index = block_ids % blk_dev
    matches = owners.reshape(-1)[:, None] == jnp.arange(peers, dtype=jnp.int32)[None, :]
    wanted = jnp.max(jnp.where(matches, local_index.reshape(-1)[:, None], 0), axis=0)
    idx = swap(wanted.reshape(peers, 1, 1))
    rows_t = prepare(table, linear, block_class)
    pulled = swap(pick(idx, rows_t))
    acc, residual = tiles(owners, values, pulled, target, gscale)
    recv = swap(acc)
    emb_grad, lin_grad = reduce_grads(idx, block_class, recv, rows_t)
    return emb_grad, lin_grad, residual


def solution(mesh):
    return jax.shard_map(
        on_device,
        mesh=mesh,
        in_specs=(
            P(AXES, None, None, None),
            P(AXES, None),
            P(AXES, None),
            P(AXES, None, None),
            P(AXES, None),
            P(AXES),
        ),
        out_specs=(P(AXES, None, None), P(AXES, None), P(AXES, None)),
        check_vma=False,
    )
```

```python
import jax
import jax.numpy as jnp
from jax import lax
from jax.experimental import pallas as pl
from jax.experimental.pallas import tpu as pltpu
from jax.sharding import PartitionSpec as P

AXES = ("group", "member")
EXTRA = 8
NT = (((1,), (1,)), ((), ()))
NN = (((1,), (0,)), ((), ()))
F32 = jnp.float32
BF16 = jnp.bfloat16


def swap(x):
    return lax.all_to_all(x, AXES, split_axis=0, concat_axis=0, tiled=True)


def prepare_body(cls_ref, table_ref, lin_ref, out_ref, lin32_ref):
    blocks, brows, cols = table_ref.shape
    lin32_ref[...] = lin_ref[...].astype(F32)
    one = lax.broadcasted_iota(jnp.int32, (cols, cols), 0)
    one = jnp.where(one == lax.broadcasted_iota(jnp.int32, (cols, cols), 1), 1.0, 0.0).astype(BF16)
    row = lax.broadcasted_iota(jnp.int32, (cols, brows), 0)
    at = lax.broadcasted_iota(jnp.int32, (EXTRA, brows), 0)

    @pl.loop(0, blocks, unroll=4)
    def _(j):
        vt = lax.dot_general(one, table_ref[j], NT, preferred_element_type=F32)
        vt = jnp.where(row < cls_ref[j], vt, 0.0)
        total = jnp.sum((vt * vt).astype(BF16).astype(F32), axis=0, keepdims=True)
        hi = total.astype(BF16).astype(F32)
        mid = (total - hi).astype(BF16).astype(F32)
        low = total - hi - mid
        extra = jnp.where(at == 0, lin32_ref[pl.ds(j, 1), :], 0.0)
        extra = jnp.where(at == 1, hi, extra)
        extra = jnp.where(at == 2, mid, extra)
        extra = jnp.where(at == 3, low, extra)
        out_ref[j] = jnp.concatenate([vt, extra], axis=0).astype(BF16)


def prepare(table, linear, block_class):
    blocks, brows, cols = table.shape
    whole = pl.BlockSpec(memory_space=pltpu.VMEM)
    return pl.pallas_call(
        prepare_body,
        in_specs=[pl.BlockSpec(memory_space=pltpu.SMEM), whole, whole],
        out_specs=whole,
        out_shape=jax.ShapeDtypeStruct((blocks, cols + EXTRA, brows), BF16),
        scratch_shapes=[pltpu.VMEM(linear.shape, F32)],
        compiler_params=pltpu.CompilerParams(vmem_limit_bytes=16 << 20),
        cost_estimate=pl.CostEstimate(flops=1 << 24, bytes_accessed=1 << 22, transcendentals=0),
        name="prepare",
    )(block_class, table, linear)


def pick_body(idx_ref, rows_ref, out_ref, flat_ref):
    @pl.loop(0, out_ref.shape[0], unroll=4)
    def _(p):
        j = idx_ref[p][0, 0]
        flat_ref[p] = j
        out_ref[p] = rows_ref[j]


def pick(idx, rows):
    peers = idx.shape[0]
    whole = pl.BlockSpec(memory_space=pltpu.VMEM)
    return pl.pallas_call(
        pick_body,
        in_specs=[whole, whole],
        out_specs=[whole, pl.BlockSpec(memory_space=pltpu.SMEM)],
        out_shape=[
            jax.ShapeDtypeStruct((peers, *rows.shape[1:]), rows.dtype),
            jax.ShapeDtypeStruct((peers,), jnp.int32),
        ],
        compiler_params=pltpu.CompilerParams(vmem_limit_bytes=24 << 20),
        name="pick",
    )(idx, rows)


def tiles_body(gscale, own_ref, x_ref, pulled_ref, target_ref, out_ref, resid_ref, acc_ref):
    step = pl.program_id(0)
    per, per_tile, tsamp, brows = x_ref.shape
    peers, rows, _ = pulled_ref.shape
    cols = rows - EXTRA

    @pl.when(step == 0)
    def _():
        @pl.loop(0, peers)
        def _(o):
            acc_ref[o] = jnp.zeros((rows, brows), F32)

    def square(x):
        return (x * x).astype(F32)

    at = lax.broadcasted_iota(jnp.int32, (EXTRA, tsamp), 0)
    left = []
    for i in range(per):
        t = step * per + i
        sums = [jnp.zeros((rows, tsamp), F32)] * 2
        squares = jnp.zeros((tsamp, brows), F32)
        for k in range(0, per_tile, 2):
            n = (k // 2) % 2
            va, vb = pulled_ref[own_ref[k, t]], pulled_ref[own_ref[k + 1, t]]
            xa, xb = x_ref[i, k], x_ref[i, k + 1]
            v = jnp.concatenate([va, vb], axis=1)
            x = jnp.concatenate([xa, xb], axis=1)
            sums[n] += lax.dot_general(v, x, NT, preferred_element_type=F32)
            for vk, xk in ((va, xa), (vb, xb)):
                rest = vk[cols:].astype(F32)
                squares += square(xk) * (rest[1:2] + rest[2:3] + rest[3:4])
        total = sums[0] + sums[1]
        main = total[:cols]
        sub = jnp.sum(squares.T, axis=0, keepdims=True)
        inter = jnp.sum(main * main, axis=0, keepdims=True)
        resid = total[cols : cols + 1] + 0.5 * (inter - sub) - target_ref[pl.ds(t, 1), :]
        resid_ref[pl.ds(t, 1), :] = resid
        scaled = resid * gscale
        lin = jnp.where(at == 0, scaled, 0.0)
        decay = jnp.where(at == 1, scaled, 0.0)
        of_x = jnp.concatenate([main * scaled, lin], axis=0).astype(BF16)
        of_sq = jnp.concatenate([jnp.zeros((cols, tsamp), F32), decay], axis=0).astype(BF16)
        left.append(jnp.concatenate([of_x, of_sq], axis=1))
    for i in range(per):
        t = step * per + i
        for k in range(0, per_tile, 2):
            x = jnp.concatenate([x_ref[i, k], x_ref[i, k + 1]], axis=1)
            both = jnp.concatenate([x, x * x], axis=0)
            term = lax.dot_general(left[i], both, NN, preferred_element_type=F32)
            acc_ref[own_ref[k, t]] += term[:, :brows]
            acc_ref[own_ref[k + 1, t]] += term[:, brows:]

    @pl.when(step == pl.num_programs(0) - 1)
    def _():
        @pl.loop(0, peers)
        def _(o):
            extra = acc_ref[o, cols:]
            hi = extra.astype(BF16).astype(F32)
            extra = hi + pltpu.roll(extra - hi, 2, 0)
            out_ref[o] = jnp.concatenate([acc_ref[o, :cols], extra], axis=0).astype(BF16)


def tiles(owners, values, pulled, target, gscale):
    n_tiles, per_tile, tsamp, brows = values.shape
    peers, rows, _ = pulled.shape
    per = 4
    return pl.pallas_call(
        lambda *refs: tiles_body(gscale, *refs),
        grid=(n_tiles // per,),
        in_specs=[
            pl.BlockSpec(memory_space=pltpu.SMEM),
            pl.BlockSpec((per, per_tile, tsamp, brows), lambda t: (t, 0, 0, 0)),
            pl.BlockSpec(memory_space=pltpu.VMEM),
            pl.BlockSpec(memory_space=pltpu.VMEM),
        ],
        out_specs=[
            pl.BlockSpec(memory_space=pltpu.VMEM),
            pl.BlockSpec(memory_space=pltpu.VMEM),
        ],
        out_shape=[
            jax.ShapeDtypeStruct((peers, rows, brows), BF16),
            jax.ShapeDtypeStruct((n_tiles, tsamp), F32),
        ],
        scratch_shapes=[pltpu.VMEM((peers, rows, brows), F32)],
        compiler_params=pltpu.CompilerParams(vmem_limit_bytes=28 << 20),
        name="tiles",
    )(owners, values, pulled, target)


def reduce_body(idx_ref, cls_ref, recv_ref, rows_ref, emb_ref, lin_ref, acc_ref, done_ref, sem):
    peers = recv_ref.shape[0]
    blocks, rows, brows = acc_ref.shape
    cols = rows - EXTRA

    @pl.loop(0, blocks)
    def _(j):
        acc_ref[j] = jnp.zeros((rows, brows), F32)

    @pl.loop(0, peers, unroll=2)
    def _(p):
        j = idx_ref[p]
        acc_ref[j] += recv_ref[p].astype(F32)

    row = lax.broadcasted_iota(jnp.int32, (cols, brows), 0)

    @pl.loop(0, blocks, unroll=2)
    def _(j):
        extra = acc_ref[j, cols:]
        lin_ref[pl.ds(j, 1), :] = extra[0:1] + extra[2:3]
        decay = extra[1:2] + extra[3:4]
        grad = acc_ref[j, :cols] - decay * rows_ref[j].astype(F32)[:cols]
        done_ref[j] = jnp.where(row < cls_ref[j], grad, 0.0).T
        pltpu.make_async_copy(done_ref.at[j], emb_ref.at[j], sem).start()

    pltpu.make_async_copy(done_ref, emb_ref, sem).wait()


def reduce_grads(idx, block_class, recv, rows_t):
    peers, rows, brows = recv.shape
    blocks = block_class.shape[0]
    cols = rows - EXTRA
    scalars = pl.BlockSpec(memory_space=pltpu.SMEM)
    whole = pl.BlockSpec(memory_space=pltpu.VMEM)
    return pl.pallas_call(
        reduce_body,
        in_specs=[scalars, scalars, whole, whole],
        out_specs=[pl.BlockSpec(memory_space=pl.ANY), whole],
        out_shape=[
            jax.ShapeDtypeStruct((blocks, brows, cols), F32),
            jax.ShapeDtypeStruct((blocks, brows), F32),
        ],
        scratch_shapes=[
            pltpu.VMEM((blocks, rows, brows), F32),
            pltpu.VMEM((blocks, brows, cols), F32),
            pltpu.SemaphoreType.DMA,
        ],
        compiler_params=pltpu.CompilerParams(vmem_limit_bytes=24 << 20),
        name="reduce_grads",
    )(idx, block_class, recv, rows_t)


def on_device(values, block_ids, target, table, linear, block_class):
    peers = lax.axis_size("group") * lax.axis_size("member")
    blk_dev = table.shape[0]
    n_tiles, per_tile, tsamp, _ = values.shape
    gscale = (tsamp * n_tiles * per_tile / blk_dev) ** (-0.5)
    ids = block_ids.T
    owners = ids // blk_dev
    local_index = (ids % blk_dev).reshape(1, 1, -1)
    matches = owners.reshape(1, 1, -1) == jnp.arange(peers, dtype=jnp.int32).reshape(peers, 1, 1)
    wanted = jnp.max(jnp.where(matches, local_index, 0), axis=2, keepdims=True)
    idx = swap(wanted)
    rows_t = prepare(table, linear, block_class)
    picked, flat = pick(idx, rows_t)
    pulled = swap(picked)
    acc, residual = tiles(owners, values, pulled, target, gscale)
    recv = swap(acc)
    emb_grad, lin_grad = reduce_grads(flat, block_class, recv, rows_t)
    return emb_grad, lin_grad, residual


def solution(mesh):
    return jax.shard_map(
        on_device,
        mesh=mesh,
        in_specs=(
            P(AXES, None, None, None),
            P(AXES, None),
            P(AXES, None),
            P(AXES, None, None),
            P(AXES, None),
            P(AXES),
        ),
        out_specs=(P(AXES, None, None), P(AXES, None), P(AXES, None)),
        check_vma=False,
    )
```

```python
import jax
import jax.numpy as jnp
from jax import lax
from jax.experimental import pallas as pl
from jax.experimental.pallas import tpu as pltpu
from jax.sharding import PartitionSpec as P

AXES = ("group", "member")
EXTRA = 8
NT = (((1,), (1,)), ((), ()))
NN = (((1,), (0,)), ((), ()))
F32 = jnp.float32
BF16 = jnp.bfloat16


def swap(x):
    return lax.all_to_all(x, AXES, split_axis=0, concat_axis=0, tiled=True)


def prepare_body(cls_ref, table_ref, lin_ref, out_ref, lin32_ref):
    blocks, brows, cols = table_ref.shape
    lin32_ref[...] = lin_ref[...].astype(F32)
    one = lax.broadcasted_iota(jnp.int32, (cols, cols), 0)
    one = jnp.where(one == lax.broadcasted_iota(jnp.int32, (cols, cols), 1), 1.0, 0.0).astype(BF16)
    row = lax.broadcasted_iota(jnp.int32, (cols, brows), 0)
    at = lax.broadcasted_iota(jnp.int32, (EXTRA, brows), 0)

    @pl.loop(0, blocks, unroll=4)
    def _(j):
        vt = lax.dot_general(one, table_ref[j], NT, preferred_element_type=F32)
        vt = jnp.where(row < cls_ref[j], vt, 0.0)
        total = jnp.sum((vt * vt).astype(BF16).astype(F32), axis=0, keepdims=True)
        hi = total.astype(BF16).astype(F32)
        mid = (total - hi).astype(BF16).astype(F32)
        low = total - hi - mid
        extra = jnp.where(at == 0, lin32_ref[pl.ds(j, 1), :], 0.0)
        extra = jnp.where(at == 1, hi, extra)
        extra = jnp.where(at == 2, mid, extra)
        extra = jnp.where(at == 3, low, extra)
        out_ref[j] = jnp.concatenate([vt, extra], axis=0).astype(BF16)


def prepare(table, linear, block_class):
    blocks, brows, cols = table.shape
    whole = pl.BlockSpec(memory_space=pltpu.VMEM)
    return pl.pallas_call(
        prepare_body,
        in_specs=[pl.BlockSpec(memory_space=pltpu.SMEM), whole, whole],
        out_specs=whole,
        out_shape=jax.ShapeDtypeStruct((blocks, cols + EXTRA, brows), BF16),
        scratch_shapes=[pltpu.VMEM(linear.shape, F32)],
        compiler_params=pltpu.CompilerParams(vmem_limit_bytes=16 << 20),
        cost_estimate=pl.CostEstimate(flops=1 << 24, bytes_accessed=1 << 22, transcendentals=0),
        name="prepare",
    )(block_class, table, linear)


def pick_body(idx_ref, rows_ref, out_ref, flat_ref):
    @pl.loop(0, out_ref.shape[0], unroll=4)
    def _(p):
        j = idx_ref[p][0, 0]
        flat_ref[p] = j
        out_ref[p] = rows_ref[j]


def pick(idx, rows):
    peers = idx.shape[0]
    whole = pl.BlockSpec(memory_space=pltpu.VMEM)
    return pl.pallas_call(
        pick_body,
        in_specs=[whole, whole],
        out_specs=[whole, pl.BlockSpec(memory_space=pltpu.SMEM)],
        out_shape=[
            jax.ShapeDtypeStruct((peers, *rows.shape[1:]), rows.dtype),
            jax.ShapeDtypeStruct((peers,), jnp.int32),
        ],
        compiler_params=pltpu.CompilerParams(vmem_limit_bytes=24 << 20),
        name="pick",
    )(idx, rows)


def tiles_body(gscale, own_ref, x_ref, pulled_ref, target_ref, out_ref, resid_ref, acc_ref):
    step = pl.program_id(0)
    per, per_tile, tsamp, brows = x_ref.shape
    peers, rows, _ = pulled_ref.shape
    cols = rows - EXTRA

    @pl.when(step == 0)
    def _():
        @pl.loop(0, peers, unroll=4)
        def _(o):
            acc_ref[o] = jnp.zeros((rows, brows), F32)

    def square(x):
        return (x * x).astype(F32)

    at = lax.broadcasted_iota(jnp.int32, (EXTRA, tsamp), 0)
    left = []
    for i in range(per):
        t = step * per + i
        sums = [jnp.zeros((rows, tsamp), F32)] * 2
        squares = jnp.zeros((tsamp, brows), F32)
        for k in range(0, per_tile, 2):
            n = (k // 2) % 2
            va, vb = pulled_ref[own_ref[k, t]], pulled_ref[own_ref[k + 1, t]]
            xa, xb = x_ref[i, k], x_ref[i, k + 1]
            v = jnp.concatenate([va, vb], axis=1)
            x = jnp.concatenate([xa, xb], axis=1)
            sums[n] += lax.dot_general(v, x, NT, preferred_element_type=F32)
            for vk, xk in ((va, xa), (vb, xb)):
                rest = vk[cols:].astype(F32)
                squares += square(xk) * (rest[1:2] + rest[2:3] + rest[3:4])
        total = sums[0] + sums[1]
        main = total[:cols]
        sub = jnp.sum(squares.T, axis=0, keepdims=True)
        inter = jnp.sum(main * main, axis=0, keepdims=True)
        resid = total[cols : cols + 1] + 0.5 * (inter - sub) - target_ref[pl.ds(t, 1), :]
        resid_ref[pl.ds(t, 1), :] = resid
        scaled = resid * gscale
        lin = jnp.where(at == 0, scaled, 0.0)
        decay = jnp.where(at == 1, scaled, 0.0)
        of_x = jnp.concatenate([main * scaled, lin], axis=0).astype(BF16)
        of_sq = jnp.concatenate([jnp.zeros((cols, tsamp), F32), decay], axis=0).astype(BF16)
        left.append(jnp.concatenate([of_x, of_sq], axis=1))
    for i in range(per):
        t = step * per + i
        for k in range(0, per_tile, 2):
            x = jnp.concatenate([x_ref[i, k], x_ref[i, k + 1]], axis=1)
            both = jnp.concatenate([x, x * x], axis=0)
            term = lax.dot_general(left[i], both, NN, preferred_element_type=F32)
            acc_ref[own_ref[k, t]] += term[:, :brows]
            acc_ref[own_ref[k + 1, t]] += term[:, brows:]

    @pl.when(step == pl.num_programs(0) - 1)
    def _():
        @pl.loop(0, peers, unroll=4)
        def _(o):
            extra = acc_ref[o, cols:]
            hi = extra.astype(BF16).astype(F32)
            extra = hi + pltpu.roll(extra - hi, 2, 0)
            out_ref[o] = jnp.concatenate([acc_ref[o, :cols], extra], axis=0).astype(BF16)


def tiles(owners, values, pulled, target, gscale):
    n_tiles, per_tile, tsamp, brows = values.shape
    peers, rows, _ = pulled.shape
    per = 4
    return pl.pallas_call(
        lambda *refs: tiles_body(gscale, *refs),
        grid=(n_tiles // per,),
        in_specs=[
            pl.BlockSpec(memory_space=pltpu.SMEM),
            pl.BlockSpec((per, per_tile, tsamp, brows), lambda t: (t, 0, 0, 0)),
            pl.BlockSpec(memory_space=pltpu.VMEM),
            pl.BlockSpec(memory_space=pltpu.VMEM),
        ],
        out_specs=[
            pl.BlockSpec(memory_space=pltpu.VMEM),
            pl.BlockSpec(memory_space=pltpu.VMEM),
        ],
        out_shape=[
            jax.ShapeDtypeStruct((peers, rows, brows), BF16),
            jax.ShapeDtypeStruct((n_tiles, tsamp), F32),
        ],
        scratch_shapes=[pltpu.VMEM((peers, rows, brows), F32)],
        compiler_params=pltpu.CompilerParams(vmem_limit_bytes=28 << 20),
        name="tiles",
    )(owners, values, pulled, target)


def reduce_body(idx_ref, cls_ref, recv_ref, rows_ref, emb_ref, lin_ref, acc_ref, done_ref, sem):
    peers = recv_ref.shape[0]
    blocks, rows, brows = acc_ref.shape
    cols = rows - EXTRA

    @pl.loop(0, blocks, unroll=4)
    def _(j):
        acc_ref[j] = jnp.zeros((rows, brows), F32)

    @pl.loop(0, peers, unroll=4)
    def _(p):
        j = idx_ref[p]
        acc_ref[j] += recv_ref[p].astype(F32)

    row = lax.broadcasted_iota(jnp.int32, (cols, brows), 0)

    @pl.loop(0, blocks, unroll=4)
    def _(j):
        extra = acc_ref[j, cols:]
        lin_ref[pl.ds(j, 1), :] = extra[0:1] + extra[2:3]
        decay = extra[1:2] + extra[3:4]
        grad = acc_ref[j, :cols] - decay * rows_ref[j].astype(F32)[:cols]
        done_ref[j] = jnp.where(row < cls_ref[j], grad, 0.0).T
        pltpu.make_async_copy(done_ref.at[j], emb_ref.at[j], sem).start()

    pltpu.make_async_copy(done_ref, emb_ref, sem).wait()


def reduce_grads(idx, block_class, recv, rows_t):
    peers, rows, brows = recv.shape
    blocks = block_class.shape[0]
    cols = rows - EXTRA
    scalars = pl.BlockSpec(memory_space=pltpu.SMEM)
    whole = pl.BlockSpec(memory_space=pltpu.VMEM)
    return pl.pallas_call(
        reduce_body,
        in_specs=[scalars, scalars, whole, whole],
        out_specs=[pl.BlockSpec(memory_space=pl.ANY), whole],
        out_shape=[
            jax.ShapeDtypeStruct((blocks, brows, cols), F32),
            jax.ShapeDtypeStruct((blocks, brows), F32),
        ],
        scratch_shapes=[
            pltpu.VMEM((blocks, rows, brows), F32),
            pltpu.VMEM((blocks, brows, cols), F32),
            pltpu.SemaphoreType.DMA,
        ],
        compiler_params=pltpu.CompilerParams(vmem_limit_bytes=24 << 20),
        name="reduce_grads",
    )(idx, block_class, recv, rows_t)


def on_device(values, block_ids, target, table, linear, block_class):
    peers = lax.axis_size("group") * lax.axis_size("member")
    blk_dev = table.shape[0]
    n_tiles, per_tile, tsamp, _ = values.shape
    gscale = (tsamp * n_tiles * per_tile / blk_dev) ** (-0.5)
    ids = block_ids.T
    owners = ids // blk_dev
    local_index = (ids % blk_dev).reshape(1, 1, -1)
    matches = owners.reshape(1, 1, -1) == jnp.arange(peers, dtype=jnp.int32).reshape(peers, 1, 1)
    wanted = jnp.max(jnp.where(matches, local_index, 0), axis=2, keepdims=True)
    idx = swap(wanted)
    rows_t = prepare(table, linear, block_class)
    picked, flat = pick(idx, rows_t)
    pulled = swap(picked)
    acc, residual = tiles(owners, values, pulled, target, gscale)
    recv = swap(acc)
    emb_grad, lin_grad = reduce_grads(flat, block_class, recv, rows_t)
    return emb_grad, lin_grad, residual


def solution(mesh):
    return jax.shard_map(
        on_device,
        mesh=mesh,
        in_specs=(
            P(AXES, None, None, None),
            P(AXES, None),
            P(AXES, None),
            P(AXES, None, None),
            P(AXES, None),
            P(AXES),
        ),
        out_specs=(P(AXES, None, None), P(AXES, None), P(AXES, None)),
        check_vma=False,
    )
```
